32 devices in a mesh: seq: 16 (over z, y, x), tp: 2 (over core).
Axes of the slice: x: 2, y: 2, z: 4, core: 2. Of those that a mesh axis runs over, the one named last changes fastest.
Arguments:
- residual_in: bfloat16 [4096, 8192], P('seq', 'tp'), may hold values from -6 to 6
- features: bfloat16 [3, 4096, 8192], P(None, 'seq', 'tp'), may hold values from -6 to 6
- short_mr: float32 [3, 7, 8192], P(None, None, 'tp'), may hold values from -2 to 2
- medium: bfloat16 [128, 512], P(None, 'tp'), may hold values from -0.5 to 0.5
- skip_mr: float32 [8192], P('tp'), may hold values from 0.5 to 1.5
- li_gates: bfloat16 [2, 4096, 8192], P(None, 'seq', 'tp'), may hold values from -6 to 6
- short_li: float32 [3, 7, 8192], P(None, None, 'tp'), may hold values from -2 to 2
- poles: float32 [16, 8192], P(None, 'tp'), may hold values from 0 to 1, as said below
- residues: float32 [16, 8192], P(None, 'tp'), may hold values from -0.5 to 0.5
- skip_li: float32 [8192], P('tp'), may hold values from 0.5 to 1.5
- w_out: bfloat16 [8192, 8192], P('seq', 'tp'), may hold values from -0.0625 to 0.0625
Outputs:
- block_out: bfloat16 [4096, 8192], P('seq', 'tp')
The draws below stay inside these ranges and needn't reach their ends.
Inputs may be any that keep to these rules, and one draw needn't show every extreme that they name: `poles`: every pole lies strictly between 0 and 1.
All inputs are finite; a program needn't handle non-finite values.
Results may differ from the reference program's by a relative error of at most 0.0064.
Values may be sent and summed in bfloat16 or wider, within the bound.
A program may use at most 384 MiB of HBM per device.

```python
import math
import jax
import jax.numpy as jnp
from jax import lax

D = 8192
MODES = 16
SHORT_TAPS = 7
MED_TAPS = 128
GROUPS = 512
TOKENS = 4096


def mode_rates(key):
    uniform_draw = jax.random.uniform(jax.random.fold_in(key, 101), (MODES, D), jnp.float32)
    slow_rate = math.log(10.0) / TOKENS
    fast_rate = 1.0 / 30.0
    lowest = math.log(slow_rate * slow_rate / fast_rate)
    return jnp.exp(lowest + uniform_draw * (math.log(fast_rate) - lowest))


def draw_poles(key, part):
    return jnp.exp(-mode_rates(key))


def draw_residues(key, part):
    rates = mode_rates(key)
    normal_draw = jax.random.truncated_normal(jax.random.fold_in(key, 103), -4.0, 4.0, (MODES, D), jnp.float32)
    return normal_draw * jnp.sqrt(2.0 * rates + 2.0 / TOKENS) * 0.25


def block_scale(stream_key, dims, split, smallest, top_value):
    loudness = 1.0
    for position, shards_of in split:
        heights = jax.random.uniform(jax.random.fold_in(jax.random.fold_in(stream_key, 6), position), (shards_of,), jnp.float32, smallest / len(split), top_value / len(split))
        loudness = loudness * jnp.repeat(jnp.exp(heights), dims[position] // shards_of).reshape((-1,) + (1,) * (len(dims) - 1 - position))
    return loudness


def normal_values(rng, dims, scale, most, cuts=(), kind=jnp.bfloat16):
    level = block_scale(rng, dims, cuts, -0.22, 0.18) if cuts else 1.0
    values = jax.random.normal(rng, dims, jnp.float32) * scale * level
    return jnp.minimum(jnp.maximum(values, -most), most).astype(kind)


def setup_inputs(seed: int = 0) -> dict:
    key_of = jax.random.split(jax.random.key(seed), 12)
    residual_in = normal_values(key_of[0], (TOKENS, D), 1.0, 6.0, ((0, 16), (1, 2)))
    features = normal_values(key_of[1], (3, TOKENS, D), 1.0, 6.0, ((1, 16), (2, 2)))
    short_mr = normal_values(key_of[2], (3, SHORT_TAPS, D), 0.4, 2.0, ((2, 2),), jnp.float32)
    medium = normal_values(key_of[3], (MED_TAPS, GROUPS), MED_TAPS ** -0.5, 0.5, ((1, 2),))
    skip_mr = jnp.clip(1.0 + 0.1 * jax.random.normal(key_of[4], (D,), jnp.float32), 0.5, 1.5)
    li_gates = normal_values(key_of[5], (2, TOKENS, D), 1.0, 6.0, ((1, 16), (2, 2)))
    short_li = normal_values(key_of[6], (3, SHORT_TAPS, D), 0.4, 2.0, ((2, 2),), jnp.float32)
    poles = draw_poles(jax.random.fold_in(key_of[11], 71), 0)
    residues = draw_residues(jax.random.fold_in(key_of[11], 71), 0)
    skip_li = jnp.clip(1.0 + 0.1 * jax.random.normal(key_of[9], (D,), jnp.float32), 0.5, 1.5)
    w_out = normal_values(key_of[10], (D, D), D ** -0.5, 0.0625, ((0, 16), (1, 2)))
    return dict(residual_in=residual_in, features=features, short_mr=short_mr, medium=medium, skip_mr=skip_mr, li_gates=li_gates, short_li=short_li, poles=poles, residues=residues, skip_li=skip_li, w_out=w_out)


block_len = 32
highest = lax.Precision.HIGHEST


def short_conv(extended, tap_table):
    rim_rows = tap_table.shape[1] - 1
    tok_rows = extended.shape[1] - rim_rows
    running = jnp.zeros((extended.shape[0], tok_rows, extended.shape[2]), jnp.float32)
    for tap_lag in range(tap_table.shape[1]):
        window = extended[:, rim_rows - tap_lag: rim_rows - tap_lag + tok_rows].astype(jnp.float32)
        running = running + tap_table[:, tap_lag][:, None, :] * window
    return running


def medium_bands(tap_table):
    length = tap_table.shape[0]
    groups = tap_table.shape[1]
    zero_rows = jnp.zeros((length - 1, groups), tap_table.dtype)
    tap_line = jnp.concatenate([zero_rows, tap_table[::-1], zero_rows], axis=0)
    bands = jnp.stack([tap_line[length - 1 - row: 3 * length - 2 - row] for row in range(length)])
    band_head = bands[:, :length]
    band_tail = jnp.concatenate([bands[:, length:], jnp.zeros((length, 1, groups), tap_table.dtype)], axis=1)
    return band_head, band_tail


def medium_conv(extended, tap_table):
    length = tap_table.shape[0]
    tok_rows = extended.shape[0] - (length - 1)
    channels = extended.shape[1]
    groups = tap_table.shape[1]
    group_width = channels // groups
    band_head, band_tail = medium_bands(tap_table)
    padded = jnp.concatenate([extended, jnp.zeros((1, channels), extended.dtype)], axis=0)
    blocks = tok_rows // length
    win_head = padded[:tok_rows].reshape(blocks, length, groups, group_width).astype(jnp.float32)
    win_tail = padded[length:tok_rows + length].reshape(blocks, length, groups, group_width).astype(jnp.float32)
    result = jnp.einsum('ijg,bjgw->bigw', band_head.astype(jnp.float32), win_head, precision=highest)
    result = result + jnp.einsum('ijg,bjgw->bigw', band_tail.astype(jnp.float32), win_tail, precision=highest)
    return result.reshape(tok_rows, channels)


def long_local(z_two, poles, residues):
    tok_rows, channels = z_two.shape
    blocks = tok_rows // block_len
    log_poles = jnp.log(poles)
    lag_steps = jnp.arange(block_len + 1).astype(jnp.float32)
    powers = jnp.exp(lag_steps[:, None, None] * log_poles[None])
    filter_taps = jnp.sum(residues[None] * powers[:block_len], axis=1)
    flipped = jnp.concatenate([filter_taps[::-1], jnp.zeros((block_len - 1, channels), jnp.float32)], axis=0)
    toeplitz = jnp.stack([flipped[block_len - 1 - row: 2 * block_len - 1 - row] for row in range(block_len)])
    pieces = z_two.reshape(blocks, block_len, channels)
    inside = jnp.einsum('ijc,njc->nic', toeplitz, pieces, precision=highest)
    block_ends = jnp.einsum('jmc,njc->nmc', powers[block_len - 1::-1], pieces, precision=highest)
    lam_block = powers[block_len]

    def advance(carried_state, block_end):
        return lam_block * carried_state + block_end, carried_state

    state_end, starts = lax.scan(advance, jnp.zeros_like(lam_block), block_ends)
    mode_gain = residues[None] * powers[1:]
    across = jnp.einsum('imc,nmc->nic', mode_gain, starts, precision=highest)
    return (inside + across).reshape(tok_rows, channels), state_end, mode_gain, log_poles


def reference(residual_in, features, short_mr, medium, skip_mr, li_gates, short_li, poles, residues, skip_li, w_out):
    rim_rows = short_mr.shape[1] - 1
    med_reach = medium.shape[0] - 1
    channels = features.shape[2]
    mr_streams = short_conv(jnp.concatenate([jnp.zeros((3, rim_rows, channels), jnp.bfloat16), features], axis=1), short_mr)
    z_one = (mr_streams[1] * mr_streams[2]).astype(jnp.bfloat16)
    medium_out = medium_conv(jnp.concatenate([jnp.zeros((med_reach, channels), jnp.bfloat16), z_one], axis=0), medium)
    y_one = (mr_streams[0] * (medium_out + skip_mr * z_one.astype(jnp.float32))).astype(jnp.bfloat16)
    li_inputs = jnp.concatenate([li_gates, y_one[None]], axis=0)
    li_streams = short_conv(jnp.concatenate([jnp.zeros((3, rim_rows, channels), jnp.bfloat16), li_inputs], axis=1), short_li)
    z_two = li_streams[1] * li_streams[2]
    long_out = long_local(z_two, poles, residues)[0]
    y_two = (li_streams[0] * (long_out + skip_li * z_two)).astype(jnp.bfloat16)
    projected = jnp.dot(y_two, w_out, preferred_element_type=jnp.float32)
    return (residual_in.astype(jnp.float32) + projected).astype(jnp.bfloat16)
```

```python
import functools
import jax
import jax.numpy as jnp
from jax import lax
from jax.experimental import pallas as pl
from jax.experimental.pallas import tpu as pltpu
from jax.sharding import PartitionSpec as P

rim = 8
inner = 4
f32 = jnp.float32
bf16 = jnp.bfloat16


def from_behind(value, axis, steps):
    count = lax.axis_size(axis)
    return lax.ppermute(value, axis, [(source, source + steps) for source in range(count - steps)])


def params():
    return pltpu.CompilerParams(
        dimension_semantics=("arbitrary",), vmem_limit_bytes=48 * 1024 * 1024
    )


def tile_of(channels, most):
    return min(channels, most)


def short_rows(window, taps, rows):
    total = taps[0:1] * window[rim : rim + rows]
    for lag in range(1, taps.shape[0]):
        total = total + taps[lag : lag + 1] * window[rim - lag : rim - lag + rows]
    return total


def window_of(front, main_ref, index, start, rows, lanes):
    if start == 0:
        body = main_ref[index, 0:rows, lanes].astype(f32)
        return jnp.concatenate([front, body], axis=0)
    body = main_ref[index, start - 16 : start + rows, lanes].astype(f32)
    return body[16 - rim :]


def gate_kernel(k_ref, v_ref, front_ref, taps_ref, z_ref, *, step):
    rows = k_ref.shape[1]
    for lane in range(0, k_ref.shape[2], 128):
        lanes = pl.ds(lane, 128)
        for start in range(0, rows, step):
            k_win = window_of(front_ref[1, :, lanes], k_ref, 0, start, step, lanes)
            v_win = window_of(front_ref[2, :, lanes], v_ref, 0, start, step, lanes)
            k_out = short_rows(k_win, taps_ref[1, :, lanes], step)
            v_out = short_rows(v_win, taps_ref[2, :, lanes], step)
            z_ref[pl.ds(start, step), lanes] = (k_out * v_out).astype(bf16)


def medium_kernel(
    q_ref, front_ref, head_ref, main_ref, med_ref, taps_ref, skip_ref, y_ref, win, wide, *, width
):
    rows = main_ref.shape[0]
    reach, groups = med_ref.shape
    lanes_all = main_ref.shape[1]
    win[0:reach] = head_ref[...].astype(f32)
    win[reach:] = main_ref[...].astype(f32)
    base = pl.program_id(0) * lanes_all
    owner = (base + lax.broadcasted_iota(jnp.int32, (groups, lanes_all), 1)) // width
    pick = (owner == lax.broadcasted_iota(jnp.int32, (groups, lanes_all), 0)).astype(bf16)
    wide[...] = jnp.dot(med_ref[...], pick, preferred_element_type=f32)

    @pl.loop(0, lanes_all // 128)
    def _(tile):
        lanes = pl.ds(pl.multiple_of(tile * 128, 128), 128)
        total = None
        for part in range(rim):
            acc = None
            for block in range(reach // rim):
                lag = block * rim + part
                first = reach - rim - block * rim
                term = wide[lag : lag + 1, lanes] * win[first : first + rows + rim, lanes]
                acc = term if acc is None else acc + term
            moved = acc[rim - part : rim - part + rows]
            total = moved if total is None else total + moved
        q_win = jnp.concatenate([front_ref[:, lanes], q_ref[0, :, lanes].astype(f32)], axis=0)
        q_out = short_rows(q_win, taps_ref[0, :, lanes], rows)
        z_one = win[reach : reach + rows, lanes]
        y_ref[:, lanes] = (q_out * (total + skip_ref[:, lanes] * z_one)).astype(bf16)


def states_kernel(
    g_ref, ylo_ref, yhi_ref, front_ref, taps_ref, poles_ref, q_ref, z_ref, end_ref, both, *, step
):
    half = ylo_ref.shape[0]
    rows = 2 * half
    both[0, 0:half] = ylo_ref[...]
    both[0, half:rows] = yhi_ref[...]
    for lane in range(0, g_ref.shape[2], 128):
        lanes = pl.ds(lane, 128)
        for start in range(0, rows, step):
            q_win = window_of(front_ref[0, :, lanes], g_ref, 0, start, step, lanes)
            k_win = window_of(front_ref[1, :, lanes], g_ref, 1, start, step, lanes)
            v_win = window_of(front_ref[2, :, lanes], both, 0, start, step, lanes)
            q_ref[pl.ds(start, step), lanes] = short_rows(q_win, taps_ref[0, :, lanes], step)
            k_out = short_rows(k_win, taps_ref[1, :, lanes], step)
            v_out = short_rows(v_win, taps_ref[2, :, lanes], step)
            z_ref[pl.ds(start, step), lanes] = k_out * v_out
    poles = poles_ref[...]

    def advance(block, state):
        z_rows = z_ref[pl.ds(pl.multiple_of(block * rim, rim), rim), :]
        for row in range(rim):
            state = poles * state + z_rows[row : row + 1]
        return state

    end_ref[...] = lax.fori_loop(0, rows // rim, advance, jnp.zeros_like(poles))


def long_kernel(z_ref, q_ref, in_ref, poles_ref, res_ref, skip_ref, y_ref):
    rows = z_ref.shape[0]
    poles = poles_ref[...]
    residues = res_ref[...]
    skip = skip_ref[...]

    def advance(block, state):
        for part in range(2):
            start = pl.multiple_of(block * 2 * rim + part * rim, rim)
            z_rows = z_ref[pl.ds(start, rim), :]
            outs = []
            for row in range(rim):
                state = poles * state + z_rows[row : row + 1]
                outs.append(jnp.sum(residues * state, axis=0, keepdims=True))
            long_out = jnp.concatenate(outs, axis=0)
            y = q_ref[pl.ds(start, rim), :] * (long_out + skip * z_rows)
            halves = y if part == 0 else jnp.concatenate([halves, y], axis=0)
        y_ref[0, pl.ds(pl.multiple_of(block * 2 * rim, 2 * rim), 2 * rim), :] = halves.astype(bf16)
        return state

    lax.fori_loop(0, rows // (2 * rim), advance, in_ref[...])


def cost(flops, bytes_moved):
    return pl.CostEstimate(flops=flops, bytes_accessed=bytes_moved, transcendentals=0)


def gate(features, front, taps):
    _, rows, channels = features.shape
    ct = tile_of(channels, 256)
    lags = taps.shape[1]
    return pl.pallas_call(
        functools.partial(gate_kernel, step=64),
        grid=(channels // ct,),
        in_specs=[
            pl.BlockSpec((1, rows, ct), lambda i: (1, 0, i)),
            pl.BlockSpec((1, rows, ct), lambda i: (2, 0, i)),
            pl.BlockSpec((3, rim, ct), lambda i: (0, 0, i)),
            pl.BlockSpec((3, lags, ct), lambda i: (0, 0, i)),
        ],
        out_specs=pl.BlockSpec((rows, ct), lambda i: (0, i)),
        out_shape=jax.ShapeDtypeStruct((rows, channels), bf16),
        compiler_params=params(),
        cost_estimate=cost(60 * rows * channels, 6 * rows * channels),
        name="gate",
    )(features, features, front, taps)


def medium(features, part, q_front, head, main, main_part, medium_taps, taps, skip):
    channels = features.shape[2]
    rows = medium_taps.shape[0]
    ct = tile_of(channels, 512)
    lags = taps.shape[1]
    groups = medium_taps.shape[1]
    return pl.pallas_call(
        functools.partial(medium_kernel, width=channels // groups),
        grid=(channels // ct,),
        in_specs=[
            pl.BlockSpec((1, rows, ct), lambda i: (0, part, i)),
            pl.BlockSpec((rim, ct), lambda i: (0, i)),
            pl.BlockSpec((rows, ct), lambda i: (0, i)),
            pl.BlockSpec((rows, ct), lambda i: (main_part, i)),
            pl.BlockSpec((rows, groups), lambda i: (0, 0)),
            pl.BlockSpec((3, lags, ct), lambda i: (0, 0, i)),
            pl.BlockSpec((1, ct), lambda i: (0, i)),
        ],
        out_specs=pl.BlockSpec((rows, ct), lambda i: (0, i)),
        out_shape=jax.ShapeDtypeStruct((rows, channels), bf16),
        scratch_shapes=[pltpu.VMEM((2 * rows, ct), f32), pltpu.VMEM((rows, ct), f32)],
        compiler_params=params(),
        cost_estimate=cost(40000 * rows * channels // 16, 8 * rows * channels),
        name="medium",
    )(features, q_front, head, main, medium_taps, taps, skip)


def states(gates, y_lo, y_hi, front, taps, poles):
    _, rows, channels = gates.shape
    ct = tile_of(channels, 512)
    lags = taps.shape[1]
    modes = poles.shape[0]
    line = lambda i: (0, i)
    cube = lambda i: (0, 0, i)
    return pl.pallas_call(
        functools.partial(states_kernel, step=64),
        grid=(channels // ct,),
        in_specs=[
            pl.BlockSpec((2, rows, ct), cube),
            pl.BlockSpec((rows // 2, ct), line),
            pl.BlockSpec((rows // 2, ct), line),
            pl.BlockSpec((3, rim, ct), cube),
            pl.BlockSpec((3, lags, ct), cube),
            pl.BlockSpec((modes, ct), line),
        ],
        out_specs=[
            pl.BlockSpec((rows, ct), line),
            pl.BlockSpec((rows, ct), line),
            pl.BlockSpec((modes, ct), line),
        ],
        out_shape=[
            jax.ShapeDtypeStruct((rows, channels), f32),
            jax.ShapeDtypeStruct((rows, channels), f32),
            jax.ShapeDtypeStruct((modes, channels), f32),
        ],
        scratch_shapes=[pltpu.VMEM((1, rows, ct), bf16)],
        compiler_params=params(),
        cost_estimate=cost(100 * rows * channels, 14 * rows * channels),
        name="states",
    )(gates, y_lo, y_hi, front, taps, poles)


def long_out(z_two, li_q, incoming, poles, residues, skip, piece, fan):
    rows, channels = z_two.shape
    modes = poles.shape[0]
    line = lambda i: (0, i)
    return pl.pallas_call(
        long_kernel,
        grid=(channels // piece,),
        in_specs=[
            pl.BlockSpec((rows, piece), line),
            pl.BlockSpec((rows, piece), line),
            pl.BlockSpec((modes, piece), line),
            pl.BlockSpec((modes, piece), line),
            pl.BlockSpec((modes, piece), line),
            pl.BlockSpec((1, piece), line),
        ],
        out_specs=pl.BlockSpec((1, rows, piece), lambda i: (i % fan, 0, i // fan)),
        out_shape=jax.ShapeDtypeStruct((fan, rows, channels // fan), bf16),
        compiler_params=params(),
        cost_estimate=cost(100 * rows * channels, 10 * rows * channels),
        name="long",
    )(z_two, li_q, incoming, poles, residues, skip)


def carried_state(state_end, poles, rows):
    count = lax.axis_size("seq")
    log_poles = jnp.log(poles)
    total = None
    for steps in range(1, min(inner, count - 1) + 1):
        term = from_behind(state_end, "seq", steps)
        if steps > 1:
            term = jnp.exp((rows * (steps - 1)) * log_poles) * term
        total = term if total is None else total + term
    window = inner
    while window < count:
        base = total
        for steps in range(window, min(window * inner, count), window):
            total = total + jnp.exp((rows * steps) * log_poles) * from_behind(base, "seq", steps)
        window *= inner
    return total


def dot(lhs, rhs):
    return jnp.dot(lhs, rhs, preferred_element_type=f32)


def swap(value, bit):
    count = lax.axis_size("seq")
    return lax.ppermute(value, "seq", [(source, source ^ bit) for source in range(count)])


def project_square(residual_in, y_fan, w_left, w_right):
    place = lax.rem(lax.axis_index("seq"), inner)
    parts = [lax.dynamic_index_in_dim(y_fan, place, 0, keepdims=False)]
    for bit in range(1, inner):
        outgoing = lax.dynamic_index_in_dim(y_fan, place ^ bit, 0, keepdims=False)
        parts.append(swap(outgoing, bit))
    mine = jnp.concatenate([parts[1], parts[3], parts[2], parts[0]], axis=0)
    other = lax.ppermute(mine, "tp", [(0, 1), (1, 0)])
    first = lax.axis_index("tp") == 0
    joined = jnp.concatenate(
        [jnp.where(first, mine, other), jnp.where(first, other, mine)], axis=1
    )
    rows = y_fan.shape[1]
    left_far = dot(joined[: 2 * rows], w_left).astype(bf16)
    right_far = dot(joined[rows : 3 * rows], w_right).astype(bf16)
    left_in = swap(left_far, 1)
    right_in = swap(right_far, 2)
    left_near = dot(joined[2 * rows :], w_left)
    right_one = dot(joined[:rows], w_right)
    right_own = dot(joined[3 * rows :], w_right)
    left_pass = (left_near[:rows] + left_in[rows:].astype(f32)).astype(bf16)
    right_pass = (right_one + right_in[:rows].astype(f32)).astype(bf16)
    left_last = swap(left_pass, 2)
    right_last = swap(right_pass, 1)
    left = left_near[rows:] + left_in[:rows].astype(f32) + left_last.astype(f32)
    right = right_own + right_in[rows:].astype(f32) + right_last.astype(f32)
    return (residual_in.astype(f32) + jnp.concatenate([left, right], axis=1)).astype(bf16)


def on_device(
    residual_in,
    features,
    short_mr,
    medium_taps,
    skip_mr,
    li_gates,
    short_li,
    poles,
    residues,
    skip_li,
    w_out,
):
    reach = medium_taps.shape[0]
    rows = features.shape[1]
    channels = features.shape[2]
    count = lax.axis_size("seq")
    blocks = channels // w_out.shape[0]
    square = lax.axis_size("tp") == 2 and count % inner == 0 and blocks % inner == 0
    if square:
        half = w_out.shape[1] // 2
        lines = [list(range(start, count, inner)) for start in range(inner)]
        gather = functools.partial(
            lax.all_gather, axis_name="seq", axis=0, tiled=True, axis_index_groups=lines
        )
        w_left = gather(w_out[:, :half])
        w_right = gather(w_out[:, half:])
    else:
        w_full = lax.all_gather(w_out, "seq", axis=0, tiled=True)
    tails = jnp.concatenate([features[:, rows - rim :], li_gates[:, rows - rim :]], axis=0)
    fronts = from_behind(tails, "seq", 1).astype(f32)
    mr_front = fronts[:3]
    skip_mr = skip_mr[None]
    z_one = gate(features, mr_front, short_mr)
    z_head = from_behind(z_one[rows - reach :], "seq", 1)
    q_mid = features[0, reach - rim : reach].astype(f32)
    y_hi = medium(features, 1, q_mid, z_one, z_one, 1, medium_taps, short_mr, skip_mr)
    y_front = from_behind(y_hi[reach - rim :], "seq", 1).astype(f32)
    y_lo = medium(features, 0, mr_front[0], z_head, z_one, 0, medium_taps, short_mr, skip_mr)
    li_front = jnp.concatenate([fronts[3:], y_front[None]], axis=0)
    li_q, z_two, state_end = states(li_gates, y_lo, y_hi, li_front, short_li, poles)
    incoming = carried_state(state_end, poles, rows)
    piece = w_out.shape[0]
    fan = inner if square else 1
    y_fan = long_out(z_two, li_q, incoming, poles, residues, skip_li[None], piece, fan)
    if square:
        return project_square(residual_in, y_fan, w_left, w_right)
    gathered = lax.all_gather(y_fan[0], "tp", axis=1, tiled=True)
    return (residual_in.astype(f32) + dot(gathered, w_full)).astype(bf16)


def solution(mesh):
    placed = (
        P("seq", "tp"),
        P(None, "seq", "tp"),
        P(None, None, "tp"),
        P(None, "tp"),
        P("tp"),
        P(None, "seq", "tp"),
        P(None, None, "tp"),
        P(None, "tp"),
        P(None, "tp"),
        P("tp"),
        P("seq", "tp"),
    )
    return jax.shard_map(
        on_device, mesh=mesh, in_specs=placed, out_specs=P("seq", "tp"), check_vma=False
    )
```

```python
import functools
import jax
import jax.numpy as jnp
from jax import lax
from jax.experimental import pallas as pl
from jax.experimental.pallas import tpu as pltpu
from jax.sharding import PartitionSpec as P

rim = 8
inner = 4
f32 = jnp.float32
bf16 = jnp.bfloat16


def from_behind(value, axis, steps):
    count = lax.axis_size(axis)
    return lax.ppermute(value, axis, [(source, source + steps) for source in range(count - steps)])


def params():
    return pltpu.CompilerParams(
        dimension_semantics=("arbitrary",), vmem_limit_bytes=48 * 1024 * 1024
    )


def tile_of(channels, most):
    return min(channels, most)


def short_rows(window, taps, rows):
    total = taps[0:1] * window[rim : rim + rows]
    for lag in range(1, taps.shape[0]):
        total = total + taps[lag : lag + 1] * window[rim - lag : rim - lag + rows]
    return total


def window_of(front, main_ref, index, start, rows, lanes):
    if start == 0:
        body = main_ref[index, 0:rows, lanes].astype(f32)
        return jnp.concatenate([front, body], axis=0)
    body = main_ref[index, start - 16 : start + rows, lanes].astype(f32)
    return body[16 - rim :]


def gate_kernel(k_ref, v_ref, front_ref, taps_ref, z_ref, *, step):
    rows = k_ref.shape[1]
    for lane in range(0, k_ref.shape[2], 128):
        lanes = pl.ds(lane, 128)
        for start in range(0, rows, step):
            k_win = window_of(front_ref[1, :, lanes], k_ref, 0, start, step, lanes)
            v_win = window_of(front_ref[2, :, lanes], v_ref, 0, start, step, lanes)
            k_out = short_rows(k_win, taps_ref[1, :, lanes], step)
            v_out = short_rows(v_win, taps_ref[2, :, lanes], step)
            z_ref[pl.ds(start, step), lanes] = (k_out * v_out).astype(bf16)


def medium_kernel(
    q_ref, front_ref, head_ref, main_ref, med_ref, taps_ref, skip_ref, y_ref, win, wide, *, width
):
    rows = main_ref.shape[0]
    reach, groups = med_ref.shape
    lanes_all = main_ref.shape[1]
    win[0:reach] = head_ref[...].astype(f32)
    win[reach:] = main_ref[...].astype(f32)
    base = pl.program_id(0) * lanes_all
    owner = (base + lax.broadcasted_iota(jnp.int32, (groups, lanes_all), 1)) // width
    pick = (owner == lax.broadcasted_iota(jnp.int32, (groups, lanes_all), 0)).astype(bf16)
    wide[...] = jnp.dot(med_ref[...], pick, preferred_element_type=f32)

    @pl.loop(0, lanes_all // 128)
    def _(tile):
        lanes = pl.ds(pl.multiple_of(tile * 128, 128), 128)
        total = None
        for part in range(rim):
            acc = None
            for block in range(reach // rim):
                lag = block * rim + part
                first = reach - rim - block * rim
                term = wide[lag : lag + 1, lanes] * win[first : first + rows + rim, lanes]
                acc = term if acc is None else acc + term
            moved = acc[rim - part : rim - part + rows]
            total = moved if total is None else total + moved
        q_win = jnp.concatenate([front_ref[:, lanes], q_ref[0, :, lanes].astype(f32)], axis=0)
        q_out = short_rows(q_win, taps_ref[0, :, lanes], rows)
        z_one = win[reach : reach + rows, lanes]
        y_ref[:, lanes] = (q_out * (total + skip_ref[:, lanes] * z_one)).astype(bf16)


def states_kernel(
    g_ref, ylo_ref, yhi_ref, front_ref, taps_ref, poles_ref, q_ref, z_ref, end_ref, both, *, step
):
    half = ylo_ref.shape[0]
    rows = 2 * half
    both[0, 0:half] = ylo_ref[...]
    both[0, half:rows] = yhi_ref[...]
    for lane in range(0, g_ref.shape[2], 128):
        lanes = pl.ds(lane, 128)
        for start in range(0, rows, step):
            q_win = window_of(front_ref[0, :, lanes], g_ref, 0, start, step, lanes)
            k_win = window_of(front_ref[1, :, lanes], g_ref, 1, start, step, lanes)
            v_win = window_of(front_ref[2, :, lanes], both, 0, start, step, lanes)
            q_ref[pl.ds(start, step), lanes] = short_rows(q_win, taps_ref[0, :, lanes], step)
            k_out = short_rows(k_win, taps_ref[1, :, lanes], step)
            v_out = short_rows(v_win, taps_ref[2, :, lanes], step)
            z_ref[pl.ds(start, step), lanes] = k_out * v_out
    poles = poles_ref[...]

    def advance(block, state):
        z_rows = z_ref[pl.ds(pl.multiple_of(block * rim, rim), rim), :]
        for row in range(rim):
            state = poles * state + z_rows[row : row + 1]
        return state

    end_ref[...] = lax.fori_loop(0, rows // rim, advance, jnp.zeros_like(poles))


def long_kernel(z_ref, q_ref, in_ref, poles_ref, res_ref, skip_ref, y_ref):
    rows = z_ref.shape[0]
    poles = poles_ref[...]
    residues = res_ref[...]
    skip = skip_ref[...]

    def advance(block, state):
        for part in range(2):
            start = pl.multiple_of(block * 2 * rim + part * rim, rim)
            z_rows = z_ref[pl.ds(start, rim), :]
            outs = []
            for row in range(rim):
                state = poles * state + z_rows[row : row + 1]
                outs.append(jnp.sum(residues * state, axis=0, keepdims=True))
            long_out = jnp.concatenate(outs, axis=0)
            y = q_ref[pl.ds(start, rim), :] * (long_out + skip * z_rows)
            halves = y if part == 0 else jnp.concatenate([halves, y], axis=0)
        y_ref[0, pl.ds(pl.multiple_of(block * 2 * rim, 2 * rim), 2 * rim), :] = halves.astype(bf16)
        return state

    lax.fori_loop(0, rows // (2 * rim), advance, in_ref[...])


def cost(flops, bytes_moved):
    return pl.CostEstimate(flops=flops, bytes_accessed=bytes_moved, transcendentals=0)


def gate(features, front, taps):
    _, rows, channels = features.shape
    ct = tile_of(channels, 256)
    lags = taps.shape[1]
    return pl.pallas_call(
        functools.partial(gate_kernel, step=64),
        grid=(channels // ct,),
        in_specs=[
            pl.BlockSpec((1, rows, ct), lambda i: (1, 0, i)),
            pl.BlockSpec((1, rows, ct), lambda i: (2, 0, i)),
            pl.BlockSpec((3, rim, ct), lambda i: (0, 0, i)),
            pl.BlockSpec((3, lags, ct), lambda i: (0, 0, i)),
        ],
        out_specs=pl.BlockSpec((rows, ct), lambda i: (0, i)),
        out_shape=jax.ShapeDtypeStruct((rows, channels), bf16),
        compiler_params=params(),
        cost_estimate=cost(60 * rows * channels, 6 * rows * channels),
        name="gate",
    )(features, features, front, taps)


def medium(features, part, q_front, head, main, main_part, medium_taps, taps, skip):
    channels = features.shape[2]
    rows = medium_taps.shape[0]
    ct = tile_of(channels, 512)
    lags = taps.shape[1]
    groups = medium_taps.shape[1]
    return pl.pallas_call(
        functools.partial(medium_kernel, width=channels // groups),
        grid=(channels // ct,),
        in_specs=[
            pl.BlockSpec((1, rows, ct), lambda i: (0, part, i)),
            pl.BlockSpec((rim, ct), lambda i: (0, i)),
            pl.BlockSpec((rows, ct), lambda i: (0, i)),
            pl.BlockSpec((rows, ct), lambda i: (main_part, i)),
            pl.BlockSpec((rows, groups), lambda i: (0, 0)),
            pl.BlockSpec((3, lags, ct), lambda i: (0, 0, i)),
            pl.BlockSpec((1, ct), lambda i: (0, i)),
        ],
        out_specs=pl.BlockSpec((rows, ct), lambda i: (0, i)),
        out_shape=jax.ShapeDtypeStruct((rows, channels), bf16),
        scratch_shapes=[pltpu.VMEM((2 * rows, ct), f32), pltpu.VMEM((rows, ct), f32)],
        compiler_params=params(),
        cost_estimate=cost(40000 * rows * channels // 16, 8 * rows * channels),
        name="medium",
    )(features, q_front, head, main, medium_taps, taps, skip)


def states(gates, y_lo, y_hi, front, taps, poles):
    _, rows, channels = gates.shape
    ct = tile_of(channels, 512)
    lags = taps.shape[1]
    modes = poles.shape[0]
    line = lambda i: (0, i)
    cube = lambda i: (0, 0, i)
    return pl.pallas_call(
        functools.partial(states_kernel, step=64),
        grid=(channels // ct,),
        in_specs=[
            pl.BlockSpec((2, rows, ct), cube),
            pl.BlockSpec((rows // 2, ct), line),
            pl.BlockSpec((rows // 2, ct), line),
            pl.BlockSpec((3, rim, ct), cube),
            pl.BlockSpec((3, lags, ct), cube),
            pl.BlockSpec((modes, ct), line),
        ],
        out_specs=[
            pl.BlockSpec((rows, ct), line),
            pl.BlockSpec((rows, ct), line),
            pl.BlockSpec((modes, ct), line),
        ],
        out_shape=[
            jax.ShapeDtypeStruct((rows, channels), f32),
            jax.ShapeDtypeStruct((rows, channels), f32),
            jax.ShapeDtypeStruct((modes, channels), f32),
        ],
        scratch_shapes=[pltpu.VMEM((1, rows, ct), bf16)],
        compiler_params=params(),
        cost_estimate=cost(100 * rows * channels, 14 * rows * channels),
        name="states",
    )(gates, y_lo, y_hi, front, taps, poles)


def long_out(z_two, li_q, incoming, poles, residues, skip, piece, fan):
    rows, channels = z_two.shape
    modes = poles.shape[0]
    line = lambda i: (0, i)
    return pl.pallas_call(
        long_kernel,
        grid=(channels // piece,),
        in_specs=[
            pl.BlockSpec((rows, piece), line),
            pl.BlockSpec((rows, piece), line),
            pl.BlockSpec((modes, piece), line),
            pl.BlockSpec((modes, piece), line),
            pl.BlockSpec((modes, piece), line),
            pl.BlockSpec((1, piece), line),
        ],
        out_specs=pl.BlockSpec((1, rows, piece), lambda i: (i % fan, 0, i // fan)),
        out_shape=jax.ShapeDtypeStruct((fan, rows, channels // fan), bf16),
        compiler_params=params(),
        cost_estimate=cost(100 * rows * channels, 10 * rows * channels),
        name="long",
    )(z_two, li_q, incoming, poles, residues, skip)


def carried_state(state_end, poles, rows):
    count = lax.axis_size("seq")
    log_poles = jnp.log(poles)
    total = None
    for steps in range(1, min(inner, count - 1) + 1):
        term = from_behind(state_end, "seq", steps)
        if steps > 1:
            term = jnp.exp((rows * (steps - 1)) * log_poles) * term
        total = term if total is None else total + term
    window = inner
    while window < count:
        base = total
        for steps in range(window, min(window * inner, count), window):
            total = total + jnp.exp((rows * steps) * log_poles) * from_behind(base, "seq", steps)
        window *= inner
    return total


def dot(lhs, rhs):
    return jnp.dot(lhs, rhs, preferred_element_type=f32)


def swap(value, bit):
    count = lax.axis_size("seq")
    return lax.ppermute(value, "seq", [(source, source ^ bit) for source in range(count)])


def square_state(state_end, poles, rows):
    count = lax.axis_size("seq")
    log_poles = jnp.log(poles)
    place = lax.rem(lax.axis_index("seq"), inner)
    inside = jnp.zeros_like(state_end)
    whole = jnp.zeros_like(state_end)
    for bit in range(inner):
        state = state_end if bit == 0 else swap(state_end, bit)
        source = place ^ bit
        lag = (rows * (inner - 1 - source)).astype(f32)
        whole = whole + jnp.exp(lag * log_poles) * state
        if bit > 0:
            ahead = place - 1 - source
            lag = (rows * jnp.maximum(ahead, 0)).astype(f32)
            inside = inside + jnp.where(ahead >= 0, jnp.exp(lag * log_poles) * state, 0.0)
    before = None
    for steps in range(1, count // inner):
        term = from_behind(whole, "seq", steps * inner)
        if steps > 1:
            term = jnp.exp((rows * inner * (steps - 1)) * log_poles) * term
        before = term if before is None else before + term
    if before is None:
        return inside
    return inside + jnp.exp((rows * place).astype(f32) * log_poles) * before


def product_kernel(x_ref, w_ref, *rest):
    out_ref = rest[-1]
    out_ref[...] = jnp.dot(
        x_ref[...], w_ref[...], preferred_element_type=f32
    ).astype(out_ref.dtype)


def product(x, w, block, first_row, row_blocks, first_column, columns, kind, after=()):
    depth = x.shape[1]
    ct = tile_of(columns, 512)
    base = first_column // ct
    return pl.pallas_call(
        product_kernel,
        grid=(columns // ct, row_blocks),
        in_specs=[
            pl.BlockSpec((block, depth), lambda j, i: (first_row + i, 0)),
            pl.BlockSpec((depth, ct), lambda j, i: (0, base + j)),
        ]
        + [pl.BlockSpec(memory_space=pl.ANY)] * len(after),
        out_specs=pl.BlockSpec((block, ct), lambda j, i: (i, j)),
        out_shape=jax.ShapeDtypeStruct((block * row_blocks, columns), kind),
        compiler_params=pltpu.CompilerParams(vmem_limit_bytes=40 * 1024 * 1024),
        cost_estimate=cost(
            2 * block * row_blocks * depth * columns, 2 * depth * columns
        ),
        name="product",
    )(x, w, *after)


def project_square(residual_in, y_fan, w_wide, w_last):
    place = lax.rem(lax.axis_index("seq"), inner)
    parts = [lax.dynamic_index_in_dim(y_fan, place, 0, keepdims=False)]
    for bit in range(1, inner):
        outgoing = lax.dynamic_index_in_dim(y_fan, place ^ bit, 0, keepdims=False)
        parts.append(swap(outgoing, bit))
    mine = jnp.concatenate([parts[1], parts[3], parts[2], parts[0]], axis=0)
    other = lax.ppermute(mine, "tp", [(0, 1), (1, 0)])
    first = lax.axis_index("tp") == 0
    joined = jnp.concatenate(
        [jnp.where(first, mine, other), jnp.where(first, other, mine)], axis=1
    )
    rows = y_fan.shape[1]

    def left_sums(far, pass_on, own):
        arrived = swap(far, 1).astype(f32)
        return (pass_on + arrived[rows:]).astype(bf16), own + arrived[:rows]

    def right_sums(far, pass_on, own):
        arrived = swap(far, 2).astype(f32)
        return (pass_on + arrived[:rows]).astype(bf16), own + arrived[rows:]

    wide = w_wide.shape[1] // 2
    far_left = product(joined, w_wide, rows, 0, 2, 0, wide, bf16)
    far_right = product(joined, w_wide, rows, 1, 2, wide, wide, bf16)
    near_left = product(joined, w_wide, rows, 2, 2, 0, wide, f32)
    near_right = product(joined, w_wide, rows, 0, 1, wide, wide, f32)
    own_right = product(joined, w_wide, rows, 3, 1, wide, wide, f32)
    left_pass, left_own = left_sums(far_left, near_left[:rows], near_left[rows:])
    right_pass, right_own = right_sums(far_right, near_right, own_right)
    left_end = swap(left_pass, 2)
    right_end = swap(right_pass, 1)
    left = left_own + left_end.astype(f32)
    right = right_own + right_end.astype(f32)
    half = w_last.shape[1] // 2
    ends = (left_end, right_end)
    far_l = product(joined, w_last, rows, 0, 2, 0, half, bf16, ends)
    far_r = product(joined, w_last, rows, 1, 2, half, half, bf16, ends)
    near_l = product(joined, w_last, rows, 2, 2, 0, half, f32)
    near_r = product(joined, w_last, rows, 0, 1, half, half, f32)
    last_r = product(joined, w_last, rows, 3, 1, half, half, f32)
    pass_l, own_l = left_sums(far_l, near_l[:rows], near_l[rows:])
    pass_r, own_r = right_sums(far_r, near_r, last_r)
    end_l = own_l + swap(pass_l, 2).astype(f32)
    end_r = own_r + swap(pass_r, 1).astype(f32)
    projected = jnp.concatenate([left, right, end_l, end_r], axis=1)
    return (residual_in.astype(f32) + projected).astype(bf16)


def on_device(
    residual_in,
    features,
    short_mr,
    medium_taps,
    skip_mr,
    li_gates,
    short_li,
    poles,
    residues,
    skip_li,
    w_out,
):
    reach = medium_taps.shape[0]
    rows = features.shape[1]
    channels = features.shape[2]
    count = lax.axis_size("seq")
    blocks = channels // w_out.shape[0]
    square = lax.axis_size("tp") == 2 and count % inner == 0 and blocks % inner == 0
    if square:
        wide = 3 * w_out.shape[1] // 8
        lines = [list(range(start, count, inner)) for start in range(inner)]
        gather = functools.partial(
            lax.all_gather, axis_name="seq", axis=0, tiled=True, axis_index_groups=lines
        )
        w_wide = gather(w_out[:, : 2 * wide])
        w_last = gather(w_out[:, 2 * wide :])
    else:
        w_full = lax.all_gather(w_out, "seq", axis=0, tiled=True)
    tails = jnp.concatenate([features[:, rows - rim :], li_gates[:, rows - rim :]], axis=0)
    fronts = from_behind(tails, "seq", 1).astype(f32)
    mr_front = fronts[:3]
    skip_mr = skip_mr[None]
    z_one = gate(features, mr_front, short_mr)
    z_head = from_behind(z_one[rows - reach :], "seq", 1)
    q_mid = features[0, reach - rim : reach].astype(f32)
    y_hi = medium(features, 1, q_mid, z_one, z_one, 1, medium_taps, short_mr, skip_mr)
    y_front = from_behind(y_hi[reach - rim :], "seq", 1).astype(f32)
    y_lo = medium(features, 0, mr_front[0], z_head, z_one, 0, medium_taps, short_mr, skip_mr)
    li_front = jnp.concatenate([fronts[3:], y_front[None]], axis=0)
    li_q, z_two, state_end = states(li_gates, y_lo, y_hi, li_front, short_li, poles)
    prefix = square_state if square else carried_state
    incoming = prefix(state_end, poles, rows)
    piece = w_out.shape[0]
    fan = inner if square else 1
    y_fan = long_out(z_two, li_q, incoming, poles, residues, skip_li[None], piece, fan)
    if square:
        return project_square(residual_in, y_fan, w_wide, w_last)
    gathered = lax.all_gather(y_fan[0], "tp", axis=1, tiled=True)
    return (residual_in.astype(f32) + dot(gathered, w_full)).astype(bf16)


def solution(mesh):
    placed = (
        P("seq", "tp"),
        P(None, "seq", "tp"),
        P(None, None, "tp"),
        P(None, "tp"),
        P("tp"),
        P(None, "seq", "tp"),
        P(None, None, "tp"),
        P(None, "tp"),
        P(None, "tp"),
        P("tp"),
        P("seq", "tp"),
    )
    return jax.shard_map(
        on_device, mesh=mesh, in_specs=placed, out_specs=P("seq", "tp"), check_vma=False
    )
```

```python
import functools
import jax
import jax.numpy as jnp
from jax import lax
from jax.experimental import pallas as pl
from jax.experimental.pallas import tpu as pltpu
from jax.sharding import PartitionSpec as P

rim = 8
inner = 4
f32 = jnp.float32
bf16 = jnp.bfloat16


def from_behind(value, axis, steps):
    count = lax.axis_size(axis)
    return lax.ppermute(value, axis, [(source, source + steps) for source in range(count - steps)])


def params():
    return pltpu.CompilerParams(
        dimension_semantics=("arbitrary",), vmem_limit_bytes=48 * 1024 * 1024
    )


def tile_of(channels, most):
    return min(channels, most)


def short_rows(window, taps, rows):
    total = taps[0:1] * window[rim : rim + rows]
    for lag in range(1, taps.shape[0]):
        total = total + taps[lag : lag + 1] * window[rim - lag : rim - lag + rows]
    return total


def window_of(front, main_ref, index, start, rows, lanes):
    if start == 0:
        body = main_ref[index, 0:rows, lanes].astype(f32)
        return jnp.concatenate([front, body], axis=0)
    body = main_ref[index, start - 16 : start + rows, lanes].astype(f32)
    return body[16 - rim :]


def gate_kernel(k_ref, v_ref, front_ref, taps_ref, z_ref, *, step):
    rows = k_ref.shape[1]
    for lane in range(0, k_ref.shape[2], 128):
        lanes = pl.ds(lane, 128)
        for start in range(0, rows, step):
            k_win = window_of(front_ref[1, :, lanes], k_ref, 0, start, step, lanes)
            v_win = window_of(front_ref[2, :, lanes], v_ref, 0, start, step, lanes)
            k_out = short_rows(k_win, taps_ref[1, :, lanes], step)
            v_out = short_rows(v_win, taps_ref[2, :, lanes], step)
            z_ref[pl.ds(start, step), lanes] = (k_out * v_out).astype(bf16)


def medium_kernel(
    q_ref, front_ref, head_ref, main_ref, med_ref, taps_ref, skip_ref, y_ref, win, wide, *, width
):
    rows = main_ref.shape[0]
    reach, groups = med_ref.shape
    lanes_all = main_ref.shape[1]
    win[0:reach] = head_ref[...].astype(f32)
    win[reach:] = main_ref[...].astype(f32)
    base = pl.program_id(0) * lanes_all
    owner = (base + lax.broadcasted_iota(jnp.int32, (groups, lanes_all), 1)) // width
    pick = (owner == lax.broadcasted_iota(jnp.int32, (groups, lanes_all), 0)).astype(bf16)
    wide[...] = jnp.dot(med_ref[...], pick, preferred_element_type=f32)

    @pl.loop(0, lanes_all // 128)
    def _(tile):
        lanes = pl.ds(pl.multiple_of(tile * 128, 128), 128)
        total = None
        for part in range(rim):
            acc = None
            for block in range(reach // rim):
                lag = block * rim + part
                first = reach - rim - block * rim
                term = wide[lag : lag + 1, lanes] * win[first : first + rows + rim, lanes]
                acc = term if acc is None else acc + term
            moved = acc[rim - part : rim - part + rows]
            total = moved if total is None else total + moved
        q_win = jnp.concatenate([front_ref[:, lanes], q_ref[0, :, lanes].astype(f32)], axis=0)
        q_out = short_rows(q_win, taps_ref[0, :, lanes], rows)
        z_one = win[reach : reach + rows, lanes]
        y_ref[:, lanes] = (q_out * (total + skip_ref[:, lanes] * z_one)).astype(bf16)


def states_kernel(
    g_ref, ylo_ref, yhi_ref, front_ref, taps_ref, poles_ref, q_ref, z_ref, end_ref, both, *, step
):
    half = ylo_ref.shape[0]
    rows = 2 * half
    both[0, 0:half] = ylo_ref[...]
    both[0, half:rows] = yhi_ref[...]
    for lane in range(0, g_ref.shape[2], 128):
        lanes = pl.ds(lane, 128)
        for start in range(0, rows, step):
            q_win = window_of(front_ref[0, :, lanes], g_ref, 0, start, step, lanes)
            k_win = window_of(front_ref[1, :, lanes], g_ref, 1, start, step, lanes)
            v_win = window_of(front_ref[2, :, lanes], both, 0, start, step, lanes)
            q_ref[pl.ds(start, step), lanes] = short_rows(q_win, taps_ref[0, :, lanes], step)
            k_out = short_rows(k_win, taps_ref[1, :, lanes], step)
            v_out = short_rows(v_win, taps_ref[2, :, lanes], step)
            z_ref[pl.ds(start, step), lanes] = k_out * v_out
    poles = poles_ref[...]

    def advance(block, state):
        z_rows = z_ref[pl.ds(pl.multiple_of(block * rim, rim), rim), :]
        for row in range(rim):
            state = poles * state + z_rows[row : row + 1]
        return state

    end_ref[...] = lax.fori_loop(0, rows // rim, advance, jnp.zeros_like(poles))


def long_kernel(z_ref, q_ref, in_ref, poles_ref, res_ref, skip_ref, y_ref):
    rows = z_ref.shape[0]
    poles = poles_ref[...]
    residues = res_ref[...]
    skip = skip_ref[...]

    def advance(block, state):
        for part in range(2):
            start = pl.multiple_of(block * 2 * rim + part * rim, rim)
            z_rows = z_ref[pl.ds(start, rim), :]
            outs = []
            for row in range(rim):
                state = poles * state + z_rows[row : row + 1]
                outs.append(jnp.sum(residues * state, axis=0, keepdims=True))
            long_out = jnp.concatenate(outs, axis=0)
            y = q_ref[pl.ds(start, rim), :] * (long_out + skip * z_rows)
            halves = y if part == 0 else jnp.concatenate([halves, y], axis=0)
        y_ref[0, pl.ds(pl.multiple_of(block * 2 * rim, 2 * rim), 2 * rim), :] = halves.astype(bf16)
        return state

    lax.fori_loop(0, rows // (2 * rim), advance, in_ref[...])


def cost(flops, bytes_moved):
    return pl.CostEstimate(flops=flops, bytes_accessed=bytes_moved, transcendentals=0)


def gate(features, front, taps):
    _, rows, channels = features.shape
    ct = tile_of(channels, 256)
    lags = taps.shape[1]
    return pl.pallas_call(
        functools.partial(gate_kernel, step=64),
        grid=(channels // ct,),
        in_specs=[
            pl.BlockSpec((1, rows, ct), lambda i: (1, 0, i)),
            pl.BlockSpec((1, rows, ct), lambda i: (2, 0, i)),
            pl.BlockSpec((3, rim, ct), lambda i: (0, 0, i)),
            pl.BlockSpec((3, lags, ct), lambda i: (0, 0, i)),
        ],
        out_specs=pl.BlockSpec((rows, ct), lambda i: (0, i)),
        out_shape=jax.ShapeDtypeStruct((rows, channels), bf16),
        compiler_params=params(),
        cost_estimate=cost(60 * rows * channels, 6 * rows * channels),
        name="gate",
    )(features, features, front, taps)


def medium(features, part, q_front, head, main, main_part, medium_taps, taps, skip):
    channels = features.shape[2]
    rows = medium_taps.shape[0]
    ct = tile_of(channels, 512)
    lags = taps.shape[1]
    groups = medium_taps.shape[1]
    return pl.pallas_call(
        functools.partial(medium_kernel, width=channels // groups),
        grid=(channels // ct,),
        in_specs=[
            pl.BlockSpec((1, rows, ct), lambda i: (0, part, i)),
            pl.BlockSpec((rim, ct), lambda i: (0, i)),
            pl.BlockSpec((rows, ct), lambda i: (0, i)),
            pl.BlockSpec((rows, ct), lambda i: (main_part, i)),
            pl.BlockSpec((rows, groups), lambda i: (0, 0)),
            pl.BlockSpec((3, lags, ct), lambda i: (0, 0, i)),
            pl.BlockSpec((1, ct), lambda i: (0, i)),
        ],
        out_specs=pl.BlockSpec((rows, ct), lambda i: (0, i)),
        out_shape=jax.ShapeDtypeStruct((rows, channels), bf16),
        scratch_shapes=[pltpu.VMEM((2 * rows, ct), f32), pltpu.VMEM((rows, ct), f32)],
        compiler_params=params(),
        cost_estimate=cost(40000 * rows * channels // 16, 8 * rows * channels),
        name="medium",
    )(features, q_front, head, main, medium_taps, taps, skip)


def states(gates, y_lo, y_hi, front, taps, poles):
    _, rows, channels = gates.shape
    ct = tile_of(channels, 512)
    lags = taps.shape[1]
    modes = poles.shape[0]
    line = lambda i: (0, i)
    cube = lambda i: (0, 0, i)
    return pl.pallas_call(
        functools.partial(states_kernel, step=64),
        grid=(channels // ct,),
        in_specs=[
            pl.BlockSpec((2, rows, ct), cube),
            pl.BlockSpec((rows // 2, ct), line),
            pl.BlockSpec((rows // 2, ct), line),
            pl.BlockSpec((3, rim, ct), cube),
            pl.BlockSpec((3, lags, ct), cube),
            pl.BlockSpec((modes, ct), line),
        ],
        out_specs=[
            pl.BlockSpec((rows, ct), line),
            pl.BlockSpec((rows, ct), line),
            pl.BlockSpec((modes, ct), line),
        ],
        out_shape=[
            jax.ShapeDtypeStruct((rows, channels), f32),
            jax.ShapeDtypeStruct((rows, channels), f32),
            jax.ShapeDtypeStruct((modes, channels), f32),
        ],
        scratch_shapes=[pltpu.VMEM((1, rows, ct), bf16)],
        compiler_params=params(),
        cost_estimate=cost(100 * rows * channels, 14 * rows * channels),
        name="states",
    )(gates, y_lo, y_hi, front, taps, poles)


def long_out(z_two, li_q, incoming, poles, residues, skip, piece, fan):
    rows, channels = z_two.shape
    modes = poles.shape[0]
    line = lambda i: (0, i)
    return pl.pallas_call(
        long_kernel,
        grid=(channels // piece,),
        in_specs=[
            pl.BlockSpec((rows, piece), line),
            pl.BlockSpec((rows, piece), line),
            pl.BlockSpec((modes, piece), line),
            pl.BlockSpec((modes, piece), line),
            pl.BlockSpec((modes, piece), line),
            pl.BlockSpec((1, piece), line),
        ],
        out_specs=pl.BlockSpec((1, rows, piece), lambda i: (i % fan, 0, i // fan)),
        out_shape=jax.ShapeDtypeStruct((fan, rows, channels // fan), bf16),
        compiler_params=params(),
        cost_estimate=cost(100 * rows * channels, 10 * rows * channels),
        name="long",
    )(z_two, li_q, incoming, poles, residues, skip)


def carried_state(state_end, poles, rows):
    count = lax.axis_size("seq")
    log_poles = jnp.log(poles)
    total = None
    for steps in range(1, min(inner, count - 1) + 1):
        term = from_behind(state_end, "seq", steps)
        if steps > 1:
            term = jnp.exp((rows * (steps - 1)) * log_poles) * term
        total = term if total is None else total + term
    window = inner
    while window < count:
        base = total
        for steps in range(window, min(window * inner, count), window):
            total = total + jnp.exp((rows * steps) * log_poles) * from_behind(base, "seq", steps)
        window *= inner
    return total


def dot(lhs, rhs):
    return jnp.dot(lhs, rhs, preferred_element_type=f32)


def swap(value, bit):
    count = lax.axis_size("seq")
    return lax.ppermute(value, "seq", [(source, source ^ bit) for source in range(count)])


def square_state(state_end, poles, rows):
    count = lax.axis_size("seq")
    log_poles = jnp.log(poles)
    place = lax.rem(lax.axis_index("seq"), inner)
    inside = jnp.zeros_like(state_end)
    whole = jnp.zeros_like(state_end)
    for bit in range(inner):
        state = state_end if bit == 0 else swap(state_end, bit)
        source = place ^ bit
        lag = (rows * (inner - 1 - source)).astype(f32)
        whole = whole + jnp.exp(lag * log_poles) * state
        if bit > 0:
            ahead = place - 1 - source
            lag = (rows * jnp.maximum(ahead, 0)).astype(f32)
            inside = inside + jnp.where(ahead >= 0, jnp.exp(lag * log_poles) * state, 0.0)
    if count == inner:
        return inside
    share = state_end.shape[1] // inner

    def quarter(value):
        return lax.dynamic_slice_in_dim(value, place * share, share, axis=1)

    part, log_part = quarter(whole), quarter(log_poles)
    before = None
    for steps in range(1, count // inner):
        term = from_behind(part, "seq", steps * inner)
        if steps > 1:
            term = jnp.exp((rows * inner * (steps - 1)) * log_part) * term
        before = term if before is None else before + term
    total = jnp.zeros_like(state_end)
    for bit in range(inner):
        piece = before if bit == 0 else swap(before, bit)
        total = lax.dynamic_update_slice_in_dim(total, piece, (place ^ bit) * share, axis=1)
    return inside + jnp.exp((rows * place).astype(f32) * log_poles) * total


def product_kernel(x_ref, w_ref, *rest):
    out_ref = rest[-1]
    out_ref[...] = jnp.dot(
        x_ref[...], w_ref[...], preferred_element_type=f32
    ).astype(out_ref.dtype)


def product(x, w, block, first_row, row_blocks, first_column, columns, kind, after=()):
    depth = x.shape[1]
    ct = tile_of(columns, 512)
    base = first_column // ct
    return pl.pallas_call(
        product_kernel,
        grid=(columns // ct, row_blocks),
        in_specs=[
            pl.BlockSpec((block, depth), lambda j, i: (first_row + i, 0)),
            pl.BlockSpec((depth, ct), lambda j, i: (0, base + j)),
        ]
        + [pl.BlockSpec(memory_space=pl.ANY)] * len(after),
        out_specs=pl.BlockSpec((block, ct), lambda j, i: (i, j)),
        out_shape=jax.ShapeDtypeStruct((block * row_blocks, columns), kind),
        compiler_params=pltpu.CompilerParams(vmem_limit_bytes=40 * 1024 * 1024),
        cost_estimate=cost(
            2 * block * row_blocks * depth * columns, 2 * depth * columns
        ),
        name="product",
    )(x, w, *after)


def project_square(residual_in, y_fan, w_wide, w_last):
    place = lax.rem(lax.axis_index("seq"), inner)
    parts = [lax.dynamic_index_in_dim(y_fan, place, 0, keepdims=False)]
    for bit in range(1, inner):
        outgoing = lax.dynamic_index_in_dim(y_fan, place ^ bit, 0, keepdims=False)
        parts.append(swap(outgoing, bit))
    mine = jnp.concatenate([parts[1], parts[3], parts[2], parts[0]], axis=0)
    other = lax.ppermute(mine, "tp", [(0, 1), (1, 0)])
    first = lax.axis_index("tp") == 0
    joined = jnp.concatenate(
        [jnp.where(first, mine, other), jnp.where(first, other, mine)], axis=1
    )
    rows = y_fan.shape[1]

    def left_sums(far, pass_on, own):
        arrived = swap(far, 1).astype(f32)
        return (pass_on + arrived[rows:]).astype(bf16), own + arrived[:rows]

    def right_sums(far, pass_on, own):
        arrived = swap(far, 2).astype(f32)
        return (pass_on + arrived[:rows]).astype(bf16), own + arrived[rows:]

    wide = w_wide.shape[1] // 2
    far_left = product(joined, w_wide, rows, 0, 2, 0, wide, bf16)
    far_right = product(joined, w_wide, rows, 1, 2, wide, wide, bf16)
    near_left = product(joined, w_wide, rows, 2, 2, 0, wide, f32)
    near_right = product(joined, w_wide, rows, 0, 1, wide, wide, f32)
    own_right = product(joined, w_wide, rows, 3, 1, wide, wide, f32)
    left_pass, left_own = left_sums(far_left, near_left[:rows], near_left[rows:])
    right_pass, right_own = right_sums(far_right, near_right, own_right)
    left_end = swap(left_pass, 2)
    right_end = swap(right_pass, 1)
    left = left_own + left_end.astype(f32)
    right = right_own + right_end.astype(f32)
    half = w_last.shape[1] // 2
    ends = (left_end, right_end)
    far_l = product(joined, w_last, rows, 0, 2, 0, half, bf16, ends)
    far_r = product(joined, w_last, rows, 1, 2, half, half, bf16, ends)
    near_l = product(joined, w_last, rows, 2, 2, 0, half, f32)
    near_r = product(joined, w_last, rows, 0, 1, half, half, f32)
    last_r = product(joined, w_last, rows, 3, 1, half, half, f32)
    pass_l, own_l = left_sums(far_l, near_l[:rows], near_l[rows:])
    pass_r, own_r = right_sums(far_r, near_r, last_r)
    end_l = own_l + swap(pass_l, 2).astype(f32)
    end_r = own_r + swap(pass_r, 1).astype(f32)
    projected = jnp.concatenate([left, right, end_l, end_r], axis=1)
    return (residual_in.astype(f32) + projected).astype(bf16)


def on_device(
    residual_in,
    features,
    short_mr,
    medium_taps,
    skip_mr,
    li_gates,
    short_li,
    poles,
    residues,
    skip_li,
    w_out,
):
    reach = medium_taps.shape[0]
    rows = features.shape[1]
    channels = features.shape[2]
    count = lax.axis_size("seq")
    blocks = channels // w_out.shape[0]
    square = lax.axis_size("tp") == 2 and count % inner == 0 and blocks % inner == 0
    if square:
        wide = 3 * w_out.shape[1] // 8
        lines = [list(range(start, count, inner)) for start in range(inner)]
        gather = functools.partial(
            lax.all_gather, axis_name="seq", axis=0, tiled=True, axis_index_groups=lines
        )
        w_wide = gather(w_out[:, : 2 * wide])
        w_last = gather(w_out[:, 2 * wide :])
    else:
        w_full = lax.all_gather(w_out, "seq", axis=0, tiled=True)
    tails = jnp.concatenate([features[:, rows - rim :], li_gates[:, rows - rim :]], axis=0)
    fronts = from_behind(tails, "seq", 1).astype(f32)
    mr_front = fronts[:3]
    skip_mr = skip_mr[None]
    z_one = gate(features, mr_front, short_mr)
    z_head = from_behind(z_one[rows - reach :], "seq", 1)
    q_mid = features[0, reach - rim : reach].astype(f32)
    y_hi = medium(features, 1, q_mid, z_one, z_one, 1, medium_taps, short_mr, skip_mr)
    y_front = from_behind(y_hi[reach - rim :], "seq", 1).astype(f32)
    y_lo = medium(features, 0, mr_front[0], z_head, z_one, 0, medium_taps, short_mr, skip_mr)
    li_front = jnp.concatenate([fronts[3:], y_front[None]], axis=0)
    li_q, z_two, state_end = states(li_gates, y_lo, y_hi, li_front, short_li, poles)
    prefix = square_state if square else carried_state
    incoming = prefix(state_end, poles, rows)
    piece = w_out.shape[0]
    fan = inner if square else 1
    y_fan = long_out(z_two, li_q, incoming, poles, residues, skip_li[None], piece, fan)
    if square:
        return project_square(residual_in, y_fan, w_wide, w_last)
    gathered = lax.all_gather(y_fan[0], "tp", axis=1, tiled=True)
    return (residual_in.astype(f32) + dot(gathered, w_full)).astype(bf16)


def solution(mesh):
    placed = (
        P("seq", "tp"),
        P(None, "seq", "tp"),
        P(None, None, "tp"),
        P(None, "tp"),
        P("tp"),
        P(None, "seq", "tp"),
        P(None, None, "tp"),
        P(None, "tp"),
        P(None, "tp"),
        P("tp"),
        P("seq", "tp"),
    )
    return jax.shard_map(
        on_device, mesh=mesh, in_specs=placed, out_specs=P("seq", "tp"), check_vma=False
    )
```
